256 devices in a mesh: seq: 64 (over z_hi, x, y, core), head: 4 (over z_lo).
Axes of the slice: x: 4, y: 4, z: 8 (z_hi: 2, z_lo: 4; z = z_hi * 4 + z_lo), core: 2. Of those that a mesh axis runs over, the one named last changes fastest.
Arguments:
- queries: bfloat16 [16384, 4096], P('seq', 'head'), may hold values from -80 to 80
- keys: bfloat16 [16384, 4096], P('seq', 'head'), may hold values from -4 to 4
- values: bfloat16 [16384, 4096], P('seq', 'head'), may hold values from -5 to 5
- layout: int32 [128, 5], P('seq'), may hold values from 0 to 1
- out_weight: bfloat16 [4096, 4096], P('head'), may hold values from -0.125 to 0.125
- out_grad: bfloat16 [16384, 4096], P('seq', 'head'), may hold values from -5 to 5
Outputs:
- mixed: bfloat16 [16384, 4096], P('seq', 'head')
- grad_queries: bfloat16 [16384, 4096], P('seq', 'head')
- grad_keys: bfloat16 [16384, 4096], P('seq', 'head')
- grad_values: bfloat16 [16384, 4096], P('seq', 'head')
The draws below stay inside these ranges and needn't reach their ends.
All inputs are finite; a program needn't handle non-finite values.
Results may differ from the reference program's by a relative error of at most 0.034.
Values may be sent and summed in bfloat16 or wider, within the bound.
No kernel may reach another device: no remote copies, remote signals or barrier semaphores. Data moves between devices by JAX's collectives and lax.ppermute only.
A program may use at most 128 MiB of HBM per device.

```python
import math
import jax
import jax.numpy as jnp
from jax import lax

HEADS = 32
HD = 128
DW = 4096
BLOCK_TOKENS = 128
LEVELS = 5
T_DEV = 256
TOKENS = 16384
NBLK = 128
N_SEQ = 64


def paired_fields(key):
    query_key = jax.random.fold_in(key, 101)
    field_key = jax.random.fold_in(key, 202)
    shape = (TOKENS, HEADS, HD)
    query = jnp.clip(jax.random.normal(query_key, shape, jnp.float32), -4.0, 4.0)
    field = jnp.clip(jax.random.normal(field_key, shape, jnp.float32), -4.0, 4.0)
    inside = jnp.arange(TOKENS) % BLOCK_TOKENS
    twin_rows = (inside == BLOCK_TOKENS - 5)[:, None, None]
    field = jnp.where(twin_rows, field, field)
    marked = (inside == BLOCK_TOKENS - 3)[:, None, None]
    query = jnp.where(marked, query, query)
    return (query.reshape(TOKENS, HEADS * HD), field.reshape(TOKENS, HEADS * HD))


def draw_queries(key, part):
    query, field = paired_fields(key)
    return query.astype(jnp.bfloat16)


def draw_keys(key, part):
    query, field = paired_fields(key)
    return field.astype(jnp.bfloat16)


def plant(values, own_key, smallest, largest):
    spot = [jax.random.randint(jax.random.fold_in(own_key, axis), (), 0, length) for axis, length in enumerate(values.shape)]
    widest = values.shape.index(max(values.shape))
    next_to = spot[:widest] + [(spot[widest] + 1) % values.shape[widest]] + spot[widest + 1:]
    return values.at[tuple(spot)].set(smallest).at[tuple(next_to)].set(largest)


def raised(result, key, source, target, parts, factor):
    def block_of(axis_at):
        return (jnp.arange(result.shape[axis_at]) // (result.shape[axis_at] // parts)).reshape((-1,) + (1,) * (result.ndim - 1 - axis_at))

    near = jax.random.permutation(key, parts)[block_of(target)]
    second = (block_of(target) + parts // 2) % parts
    return jnp.where((block_of(source) == near) | (block_of(source) == second), factor * result, result)


def steps_of(rng, dims, pieces, low, largest):
    gain, own = 1.0, jax.random.fold_in(rng, 6)
    for axis_at, blocks in pieces:
        draws = jnp.exp(jax.random.uniform(jax.random.fold_in(own, axis_at), (blocks,), jnp.float32, low / len(pieces), largest / len(pieces)))
        gain = gain * jnp.repeat(draws, dims[axis_at] // blocks).reshape([-1 if axis == axis_at else 1 for axis in range(len(dims))])
    return gain


def centred(rng, extent, spread, limit, cuts=(), held_as=jnp.bfloat16):
    drawn = jax.random.normal(rng, extent, jnp.float32) * spread
    if len(cuts) > 0:
        drawn = steps_of(rng, extent, cuts, -0.22, 0.18) * drawn
    return jnp.clip(drawn, min=-limit, max=limit).astype(held_as)


def bell_draw_with(stream_key, shape, width, bound, cuts, heavy, kind=jnp.bfloat16):
    entries = width * jax.random.normal(stream_key, shape, jnp.float32)
    if cuts:
        entries = entries * steps_of(stream_key, shape, cuts, -0.22, 0.18)
    return jnp.clip(raised(entries, jax.random.fold_in(stream_key, 3), *heavy), -bound, bound).astype(kind)


def setup_inputs(seed: int = 0) -> dict:
    key_of = jax.random.split(jax.random.key(seed), 7)
    queries = draw_queries(jax.random.fold_in(key_of[6], 71), 0)
    keys = draw_keys(jax.random.fold_in(key_of[6], 71), 0)
    values = centred(key_of[2], (TOKENS, HEADS * HD), 1.0, 5.0, ((0, 64), (1, 4)))
    layout = plant(jax.random.randint(key_of[3], (NBLK, LEVELS), 0, T_DEV // BLOCK_TOKENS), jax.random.fold_in(key_of[3], 1), 0, (T_DEV // BLOCK_TOKENS) - 1).astype(jnp.int32)
    out_weight = bell_draw_with(key_of[4], (HEADS * HD, DW), (HEADS * HD) ** -0.5, 0.125, ((0, 4),), (0, 1, 4, 2.0))
    out_grad = centred(key_of[5], (TOKENS, DW), 1.0, 5.0, ((0, 64), (1, 4)))
    return {"queries": queries, "keys": keys, "values": values, "layout": layout, "out_weight": out_weight, "out_grad": out_grad}


def reference(queries, keys, values, layout, out_weight, out_grad):
    per_device = T_DEV // BLOCK_TOKENS
    count_of_blocks = TOKENS // BLOCK_TOKENS
    logit_scale = 1.0 / math.sqrt(HD)
    exponents = [e for e in range(LEVELS) if 2 ** e < N_SEQ]
    head_width = len(exponents)
    owner = jnp.arange(count_of_blocks, dtype=jnp.int32) // per_device
    source_list = []
    present_list = []
    for exponent in exponents:
        reach = 2 ** exponent
        alive = owner >= reach
        source = jnp.where(alive, (owner - reach) * per_device + layout[:, exponent], 0).astype(jnp.int32)
        source_list.append(source)
        present_list.append(alive)
    sources = jnp.stack(source_list, 1)
    present = jnp.stack(present_list, 1)
    causal = jnp.tril(jnp.ones((BLOCK_TOKENS, BLOCK_TOKENS), bool))
    near_allowed = jnp.broadcast_to(causal[None], (count_of_blocks, BLOCK_TOKENS, BLOCK_TOKENS))
    far_allowed = jnp.broadcast_to(present[:, None, :, None], (count_of_blocks, BLOCK_TOKENS, head_width, BLOCK_TOKENS)).reshape(count_of_blocks, BLOCK_TOKENS, head_width * BLOCK_TOKENS)
    allowed = jnp.concatenate([near_allowed, far_allowed], -1)
    grad_attn = jnp.dot(out_grad, out_weight.T, preferred_element_type=jnp.float32).astype(jnp.bfloat16)

    def heads_major(x):
        return x.reshape(count_of_blocks, BLOCK_TOKENS, HEADS, HD).transpose(2, 0, 1, 3)

    def one_head(stacked):
        query, key_rows, value_rows, grad_rows = stacked
        query_single = query.astype(jnp.float32)
        key_single = key_rows.astype(jnp.float32)
        value_single = value_rows.astype(jnp.float32)
        gradient_single = grad_rows.astype(jnp.float32)
        distant_keys = key_single[sources]
        distant_values = value_single[sources]
        local_scores = jnp.einsum('xtz,xsz->xts', query_single, key_single) * logit_scale
        distant_scores = jnp.einsum('tei,tyhi->teyh', query_single, distant_keys).reshape(count_of_blocks, BLOCK_TOKENS, head_width * BLOCK_TOKENS) * logit_scale
        scores = jnp.concatenate([local_scores, distant_scores], -1)
        row_peak = lax.optimization_barrier(jnp.max(jnp.where(allowed, scores, -jnp.inf), -1, keepdims=True))
        weights_raw = jnp.where(allowed, jnp.exp(scores - row_peak), 0.0)
        probs = weights_raw / lax.optimization_barrier(jnp.sum(weights_raw, -1, keepdims=True))
        probs_low = probs.astype(jnp.bfloat16).astype(jnp.float32)
        local_precise = probs_low[..., :BLOCK_TOKENS]
        distant_precise = probs_low[..., BLOCK_TOKENS:].reshape(count_of_blocks, BLOCK_TOKENS, head_width, BLOCK_TOKENS)
        sparse_attention = (jnp.einsum('pzf,pfs->pzs', local_precise, value_single) + jnp.einsum('hpax,haxz->hpz', distant_precise, distant_values)).astype(jnp.bfloat16)
        correction = lax.optimization_barrier(jnp.sum(gradient_single * sparse_attention.astype(jnp.float32), -1))[..., None]
        local_prob_gradient = jnp.einsum('xtz,xsz->xts', gradient_single, value_single)
        distant_prob_gradient = jnp.einsum('tei,tyhi->teyh', gradient_single, distant_values).reshape(count_of_blocks, BLOCK_TOKENS, head_width * BLOCK_TOKENS)
        dprob = jnp.concatenate([local_prob_gradient, distant_prob_gradient], -1)
        grad_scores = (probs * (dprob - correction) * logit_scale).astype(jnp.bfloat16).astype(jnp.float32)
        local_gradient = grad_scores[..., :BLOCK_TOKENS]
        distant_gradient = grad_scores[..., BLOCK_TOKENS:].reshape(count_of_blocks, BLOCK_TOKENS, head_width, BLOCK_TOKENS)
        query_gradient = jnp.einsum('pzf,pfs->pzs', local_gradient, key_single) + jnp.einsum('hpax,haxz->hpz', distant_gradient, distant_keys)
        key_gradient_sum = jnp.einsum('ohe,ohm->oem', local_gradient, query_single)
        value_gradient_sum = jnp.einsum('ohe,ohm->oem', local_precise, gradient_single)
        distant_key_parts = jnp.einsum('gmcu,gmh->gcuh', distant_gradient, query_single)
        distant_value_parts = jnp.einsum('gmcu,gmh->gcuh', distant_precise, gradient_single)
        slots = jnp.arange(per_device, dtype=jnp.int32)
        for index, exponent in enumerate(exponents):
            reach = 2 ** exponent
            pick_mask = (layout[:, exponent].reshape(N_SEQ, per_device)[:, :, None] == slots[None, None, :]).astype(jnp.float32)
            pick_mask = pick_mask[:, :, :, None, None]
            both = []
            for terms in (distant_key_parts, distant_value_parts):
                grouped = terms[:, index].reshape(N_SEQ, per_device, 1, BLOCK_TOKENS, HD)
                summed = lax.optimization_barrier(jnp.sum(pick_mask * grouped, 1)).astype(jnp.bfloat16).astype(jnp.float32)
                moved = jnp.concatenate([summed[reach:], jnp.zeros((reach, per_device, BLOCK_TOKENS, HD), jnp.float32)], 0)
                both.append(moved.reshape(count_of_blocks, BLOCK_TOKENS, HD))
            key_gradient_sum = key_gradient_sum + both[0]
            value_gradient_sum = value_gradient_sum + both[1]
        return (sparse_attention, query_gradient.astype(jnp.bfloat16), key_gradient_sum.astype(jnp.bfloat16), value_gradient_sum.astype(jnp.bfloat16))
    results = lax.map(one_head, (heads_major(queries), heads_major(keys), heads_major(values), heads_major(grad_attn)))

    def token_major(x):
        return x.transpose(1, 2, 0, 3).reshape(TOKENS, HEADS * HD)
    attention_all = token_major(results[0])
    mixed = jnp.dot(attention_all, out_weight, preferred_element_type=jnp.float32).astype(jnp.bfloat16)
    return (mixed, token_major(results[1]), token_major(results[2]), token_major(results[3]))
```

```python
import math

import jax
import jax.numpy as jnp
from jax import lax
from jax.experimental import pallas as pl
from jax.experimental.pallas import tpu as pltpu
from jax.sharding import PartitionSpec as P

HD = 128
BT = 128
LEVELS = 5
SCALE = 1.0 / math.sqrt(HD)
LOG2E = 1.0 / math.log(2.0)
NEG = -1e30
BF = jnp.bfloat16
F32 = jnp.float32
RUNS = 64
GROUPS = 4
NT = (((1,), (1,)), ((), ()))
NN = (((1,), (0,)), ((), ()))
TN = (((0,), (0,)), ((), ()))


def params(mib=48):
    return pltpu.CompilerParams(vmem_limit_bytes=mib * 1024 * 1024)


def dot(a, b, dims):
    return lax.dot_general(a, b, dims, preferred_element_type=F32)


def move(value, target):
    pairs = [(r, target(r)) for r in range(RUNS)]
    return lax.ppermute(value, "seq", [(a, b) for a, b in pairs if b is not None])


def x_of(r):
    return (r >> 3) & 3


def gather_blocks(meta, refs, t, b):
    own = refs[0][t, b * BT : (b + 1) * BT, :]
    far = [refs[1 + j][t, pl.ds(pl.multiple_of(meta[b * LEVELS + j] * BT, BT), BT), :] for j in range(LEVELS)]
    return jnp.concatenate([own] + far, axis=0)


def forward_kernel(meta, q, *refs):
    pairs, (p_out, o_out) = refs[:6], refs[6:]
    position = meta[2 * LEVELS]
    rows = lax.broadcasted_iota(jnp.int32, (BT, BT), 0)
    cols = lax.broadcasted_iota(jnp.int32, (BT, BT), 1)
    for b in range(2):
        mine = slice(b * BT, (b + 1) * BT)
        s = dot(q[mine, :], gather_blocks(meta, pairs, 0, b), NT)
        parts = [jnp.where(rows >= cols, s[:, :BT], NEG)]
        for j in range(LEVELS):
            parts.append(jnp.where(position >= 2**j, s[:, (j + 1) * BT : (j + 2) * BT], NEG))
        s = jnp.concatenate(parts, axis=1)
        peak = jnp.max(s, axis=1, keepdims=True)
        e = jnp.exp2((s - peak) * (SCALE * LOG2E))
        p = (e * (1.0 / jnp.sum(e, axis=1, keepdims=True))).astype(BF)
        p_out[0, mine, :] = p
        o_out[mine, :] = dot(p, gather_blocks(meta, pairs, 1, b), NN).astype(BF)


def forward(meta, queries, pairs):
    heads = queries.shape[1] // HD
    col = pl.BlockSpec((2 * BT, HD), lambda h, m: (0, h))
    both = pl.BlockSpec((2, 2 * BT, HD), lambda h, m: (0, 0, h))
    return pl.pallas_call(
        forward_kernel,
        grid_spec=pltpu.PrefetchScalarGridSpec(
            num_scalar_prefetch=1,
            grid=(heads,),
            in_specs=[col] + [both] * 6,
            out_specs=[pl.BlockSpec((1, 2 * BT, 6 * BT), lambda h, m: (h, 0, 0)), col],
        ),
        out_shape=[
            jax.ShapeDtypeStruct((heads, 2 * BT, 6 * BT), BF),
            jax.ShapeDtypeStruct(queries.shape, BF),
        ],
        compiler_params=params(),
        cost_estimate=pl.CostEstimate(flops=10**9, bytes_accessed=9 * 2**20, transcendentals=10**6),
        name="attend",
    )(meta, queries, *pairs)


def backward_kernel(meta, q, g, o, p_in, *refs):
    pairs, (dq_out, own_out), sends = refs[:6], refs[6:8], refs[8:]
    halves = []
    for b in range(2):
        mine = slice(b * BT, (b + 1) * BT)
        gb = g[mine, :]
        qb = q[mine, :]
        correction = jnp.sum(gb.astype(F32) * o[mine, :].astype(F32), axis=1, keepdims=True)
        p = p_in[0, mine, :]
        dp = dot(gb, gather_blocks(meta, pairs, 1, b), NT)
        ds = (p.astype(F32) * (dp - correction) * SCALE).astype(BF)
        dq_out[mine, :] = dot(ds, gather_blocks(meta, pairs, 0, b), NN).astype(BF)
        dk = dot(ds, qb, TN)
        dv = dot(p, gb, TN)
        own_out[0, mine, :] = dk[:BT]
        own_out[1, mine, :] = dv[:BT]
        halves.append((dk, dv))
    for j in range(LEVELS):
        part = slice((j + 1) * BT, (j + 2) * BT)
        for t in range(2):
            for slot in range(2):
                total = jnp.where(meta[j] == slot, halves[0][t][part], 0.0) + jnp.where(
                    meta[LEVELS + j] == slot, halves[1][t][part], 0.0
                )
                rows = slice(slot * BT, (slot + 1) * BT)
                if j < 3:
                    sends[j][t, rows, :] = total.astype(BF)
                else:
                    sends[3 + 2 * (j - 3) + t][rows, :] = total.astype(BF)


def backward(meta, queries, grads, attended, probs, pairs):
    heads = queries.shape[1] // HD
    col = pl.BlockSpec((2 * BT, HD), lambda h, m: (0, h))
    both = pl.BlockSpec((2, 2 * BT, HD), lambda h, m: (0, 0, h))
    pair = (2,) + queries.shape
    return pl.pallas_call(
        backward_kernel,
        grid_spec=pltpu.PrefetchScalarGridSpec(
            num_scalar_prefetch=1,
            grid=(heads,),
            in_specs=[col] * 3 + [pl.BlockSpec((1, 2 * BT, 6 * BT), lambda h, m: (h, 0, 0))] + [both] * 6,
            out_specs=[col, both] + [both] * 3 + [col] * 4,
        ),
        out_shape=[jax.ShapeDtypeStruct(queries.shape, BF), jax.ShapeDtypeStruct(pair, F32)]
        + [jax.ShapeDtypeStruct(pair, BF)] * 3
        + [jax.ShapeDtypeStruct(queries.shape, BF)] * 4,
        compiler_params=params(),
        cost_estimate=pl.CostEstimate(flops=2 * 10**9, bytes_accessed=19 * 2**20, transcendentals=0),
        name="attend_back",
    )(meta, queries, grads, attended, probs, *pairs)


def project_back_kernel(g, w, out):
    out[...] = dot(g[...], w[...], NT).astype(BF)


def project_back(grads, weight):
    tokens = grads.shape[0]
    tile = 256
    return pl.pallas_call(
        project_back_kernel,
        grid=(weight.shape[0] // tile,),
        in_specs=[
            pl.BlockSpec(grads.shape, lambda i: (0, 0)),
            pl.BlockSpec((tile, weight.shape[1]), lambda i: (i, 0)),
        ],
        out_specs=pl.BlockSpec((tokens, tile), lambda i: (0, i)),
        out_shape=jax.ShapeDtypeStruct((tokens, weight.shape[0]), BF),
        compiler_params=params(),
        cost_estimate=pl.CostEstimate(flops=2 * 10**9, bytes_accessed=10 * 2**20, transcendentals=0),
        name="project_back",
    )(grads, weight)


def project_kernel(a, w, out):
    out[...] = dot(a[...], w[...], NN).astype(BF)


def project(attended, weight):
    tokens, depth = attended.shape
    wide = weight.shape[1] // GROUPS
    tile = 512
    steps = wide // tile
    return pl.pallas_call(
        project_kernel,
        grid=(GROUPS * steps,),
        in_specs=[
            pl.BlockSpec((tokens, depth), lambda i: (0, 0)),
            pl.BlockSpec((depth, tile), lambda i: (0, i)),
        ],
        out_specs=pl.BlockSpec((tokens, tile), lambda i: (i // steps, i % steps)),
        out_shape=jax.ShapeDtypeStruct((GROUPS * tokens, wide), BF),
        compiler_params=params(),
        cost_estimate=pl.CostEstimate(flops=2 * 10**9, bytes_accessed=11 * 2**20, transcendentals=0),
        name="project",
    )(attended, weight)


def nothing(*refs):
    pass


def after(value, *others):
    anywhere = pl.BlockSpec(memory_space=pl.ANY)
    return pl.pallas_call(
        nothing,
        in_specs=[anywhere] * (1 + len(others)),
        out_specs=anywhere,
        out_shape=jax.ShapeDtypeStruct(value.shape, value.dtype),
        input_output_aliases={0: 0},
        cost_estimate=pl.CostEstimate(flops=0, bytes_accessed=0, transcendentals=0),
        name="after",
    )(value, *others)


def body(queries, keys, values, layout, out_weight, out_grad):
    position = lax.axis_index("seq").astype(jnp.int32)
    meta = jnp.concatenate([layout.reshape(-1), position[None]])
    inside = position % 8
    octet = position // 8
    core = position % 2

    pair = jnp.stack([keys, values])
    r16 = move(pair, lambda r: r + 16 if r < 48 else None)
    r8o = move(pair, lambda r: r + 8 if x_of(r) < 3 else None)
    r2o = move(pair, lambda r: r + 2 if r % 8 < 6 else None)
    r4o = move(pair, lambda r: r + 4 if r % 8 < 4 else None)
    r16 = after(r16, r8o, r2o, r4o)
    full_grad = lax.all_gather(after(out_grad, r16), "head", axis=1, tiled=True)
    r8w = move(r16, lambda r: r - 8 if 40 <= r < 48 else None)
    r8 = jnp.where(octet == 4, r8w, r8o)
    r2w = move(r8, lambda r: r - 6 if r % 8 >= 6 else None)
    r4w = move(r8, lambda r: r - 4 if r % 8 >= 4 else None)
    r2 = jnp.where(inside < 2, r2w, r2o)
    r4 = jnp.where(inside < 4, r4w, r4o)
    r1 = move(jnp.where(core == 0, pair, r2), lambda r: r ^ 1)
    pairs = (pair, r1, r2, r4, r8, r16)
    probs, attended = forward(meta, queries, pairs)
    partial = project(attended, out_weight)
    mixed = lax.psum_scatter(partial, "head", scatter_dimension=0, tiled=True)
    grad_attn = project_back(after(full_grad, partial), out_weight)
    dq, own, g1, g2, g4, k8, v8, k16, v16 = backward(meta, queries, grad_attn, attended, probs, pairs)

    crossing = lambda r: r - 16 if 32 <= r < 48 else None
    within = lambda r: r - 16 if x_of(r) >= 2 else None
    near = lambda r: r - 8 if x_of(r) > 0 else None
    s1 = move(g1, lambda r: r ^ 1)
    w4 = move(g4, lambda r: r + 4 if r % 8 < 4 else None)
    xv16 = move(v16, lambda r: r + 16 if 32 <= r < 48 else None)
    zk16 = move(k16, crossing)
    g2 = (g2.astype(F32) + jnp.where(core == 1, s1, 0).astype(F32)).astype(BF)
    w2 = move(g2, lambda r: r + 6 if r % 8 < 2 else None)
    zv16 = move(xv16, lambda r: r - 32 if r >= 48 else None)
    h4 = move(g4, lambda r: r - 4 if r % 8 >= 4 else None)
    h2 = move(g2, lambda r: r - 2 if r % 8 >= 2 else None)
    h16 = [move(k16, within), move(v16, within)]
    w2 = after(w2, *h16)
    k8 = (k8.astype(F32) + w2[0].astype(F32) + w4[0].astype(F32)).astype(BF)
    v8 = (v8.astype(F32) + w2[1].astype(F32) + w4[1].astype(F32)).astype(BF)
    xv8 = move(v8, lambda r: r + 24 if 32 <= r < 40 else None)
    zk8 = move(k8, lambda r: r - 8 if 32 <= r < 40 else None)
    h8 = [move(k8, near), move(v8, near)]
    xv8 = after(xv8, h4, h2, zk16, zv16)
    zv8 = move(xv8, lambda r: r - 32 if r >= 56 else None)
    early = own + jnp.where(core == 0, s1, 0).astype(F32) + h4.astype(F32) + h2.astype(F32)
    totals = []
    for t, terms in ((0, (zk16, h16[0], h8[0], zk8)), (1, (zv16, h16[1], h8[1], zv8))):
        total = early[t]
        for term in terms:
            total = total + term.astype(F32)
        totals.append(total.astype(BF))
    return mixed, dq, totals[0], totals[1]


def solution(mesh):
    placed = (
        P("seq", "head"),
        P("seq", "head"),
        P("seq", "head"),
        P("seq", None),
        P("head", None),
        P("seq", "head"),
    )
    return jax.shard_map(
        body,
        mesh=mesh,
        in_specs=placed,
        out_specs=(P("seq", "head"), P("seq", "head"), P("seq", "head"), P("seq", "head")),
        check_vma=False,
    )
```

```python
import math

import jax
import jax.numpy as jnp
from jax import lax
from jax.experimental import pallas as pl
from jax.experimental.pallas import tpu as pltpu
from jax.sharding import PartitionSpec as P

HD = 128
BT = 128
LEVELS = 5
SCALE = 1.0 / math.sqrt(HD)
LOG2E = 1.0 / math.log(2.0)
NEG = -1e30
BF = jnp.bfloat16
F32 = jnp.float32
RUNS = 64
GROUPS = 4
STEP = 2
NT = (((1,), (1,)), ((), ()))
NN = (((1,), (0,)), ((), ()))
TN = (((0,), (0,)), ((), ()))


def params(mib=48):
    return pltpu.CompilerParams(vmem_limit_bytes=mib * 1024 * 1024)


def dot(a, b, dims):
    return lax.dot_general(a, b, dims, preferred_element_type=F32)


def move(value, target):
    pairs = [(r, target(r)) for r in range(RUNS)]
    return lax.ppermute(value, "seq", [(a, b) for a, b in pairs if b is not None])


def x_of(r):
    return (r >> 3) & 3


KEY_REFS = (1, 1, 2, 2, 1, 1)
VALUE_REFS = (1, 1, 2, 2, 1, 2)


def grouped(refs, counts):
    groups, at = [], 0
    for count in counts:
        groups.append(refs[at : at + count])
        at += count
    return groups


def gather_blocks(meta, groups, b, cols):
    blocks = [groups[0][0][b * BT : (b + 1) * BT, cols]]
    for j in range(LEVELS):
        rows = pl.ds(pl.multiple_of(meta[b * LEVELS + j] * BT, BT), BT)
        block = groups[1 + j][0][rows, cols]
        if len(groups[1 + j]) == 2:
            block = block + groups[1 + j][1][rows, cols]
        blocks.append(block)
    return jnp.concatenate(blocks, axis=0)


def forward_kernel(meta, q, *refs):
    keys, values = grouped(refs[:8], KEY_REFS), grouped(refs[8:17], VALUE_REFS)
    p_out, o_out = refs[17:]
    position = meta[2 * LEVELS]
    rows = lax.broadcasted_iota(jnp.int32, (BT, BT), 0)
    cols = lax.broadcasted_iota(jnp.int32, (BT, BT), 1)
    for h, b in [(h, b) for h in range(STEP) for b in range(2)]:
        mine = slice(b * BT, (b + 1) * BT)
        here = slice(h * HD, (h + 1) * HD)
        s = dot(q[mine, here], gather_blocks(meta, keys, b, here), NT)
        parts = [jnp.where(rows >= cols, s[:, :BT], NEG)]
        for j in range(LEVELS):
            parts.append(jnp.where(position >= 2**j, s[:, (j + 1) * BT : (j + 2) * BT], NEG))
        s = jnp.concatenate(parts, axis=1)
        peak = jnp.max(s, axis=1, keepdims=True)
        e = jnp.exp2((s - peak) * (SCALE * LOG2E))
        p = (e * (1.0 / jnp.sum(e, axis=1, keepdims=True))).astype(BF)
        p_out[h, mine, :] = p
        o_out[mine, here] = dot(p, gather_blocks(meta, values, b, here), NN).astype(BF)


def forward(meta, queries, keys, values):
    heads = queries.shape[1] // HD
    col = pl.BlockSpec((2 * BT, STEP * HD), lambda h, m: (0, h))
    return pl.pallas_call(
        forward_kernel,
        grid_spec=pltpu.PrefetchScalarGridSpec(
            num_scalar_prefetch=1,
            grid=(heads // STEP,),
            in_specs=[col] * 18,
            out_specs=[pl.BlockSpec((STEP, 2 * BT, 6 * BT), lambda h, m: (h, 0, 0)), col],
        ),
        out_shape=[
            jax.ShapeDtypeStruct((heads, 2 * BT, 6 * BT), BF),
            jax.ShapeDtypeStruct(queries.shape, BF),
        ],
        compiler_params=params(),
        cost_estimate=pl.CostEstimate(flops=10**9, bytes_accessed=9 * 2**20, transcendentals=10**6),
        name="attend",
    )(meta, queries, *keys, *values)


def backward_kernel(meta, q, g, o, p_in, *refs):
    keys, values = grouped(refs[:8], KEY_REFS), grouped(refs[8:17], VALUE_REFS)
    (dq_out, own_out), sends = refs[17:19], refs[19:]
    for h in range(STEP):
        here = slice(h * HD, (h + 1) * HD)
        halves = []
        for b in range(2):
            mine = slice(b * BT, (b + 1) * BT)
            gb = g[mine, here]
            qb = q[mine, here]
            correction = jnp.sum(gb.astype(F32) * o[mine, here].astype(F32), axis=1, keepdims=True)
            p = p_in[h, mine, :]
            dp = dot(gb, gather_blocks(meta, values, b, here), NT)
            ds = (p.astype(F32) * (dp - correction) * SCALE).astype(BF)
            dq_out[mine, here] = dot(ds, gather_blocks(meta, keys, b, here), NN).astype(BF)
            dk = dot(ds, qb, TN)
            dv = dot(p, gb, TN)
            own_out[0, mine, here] = dk[:BT]
            own_out[1, mine, here] = dv[:BT]
            halves.append((dk, dv))
        for j in range(LEVELS):
            part = slice((j + 1) * BT, (j + 2) * BT)
            for t in range(2):
                for slot in range(2):
                    total = jnp.where(meta[j] == slot, halves[0][t][part], 0.0) + jnp.where(
                        meta[LEVELS + j] == slot, halves[1][t][part], 0.0
                    )
                    rows = slice(slot * BT, (slot + 1) * BT)
                    if j < 3:
                        sends[j][t, rows, here] = total.astype(BF)
                    else:
                        sends[3 + 2 * (j - 3) + t][rows, here] = total.astype(BF)


def backward(meta, queries, grads, attended, probs, keys, values):
    heads = queries.shape[1] // HD
    col = pl.BlockSpec((2 * BT, STEP * HD), lambda h, m: (0, h))
    both = pl.BlockSpec((2, 2 * BT, STEP * HD), lambda h, m: (0, 0, h))
    pair = (2,) + queries.shape
    return pl.pallas_call(
        backward_kernel,
        grid_spec=pltpu.PrefetchScalarGridSpec(
            num_scalar_prefetch=1,
            grid=(heads // STEP,),
            in_specs=[col] * 3
            + [pl.BlockSpec((STEP, 2 * BT, 6 * BT), lambda h, m: (h, 0, 0))]
            + [col] * 17,
            out_specs=[col, both] + [both] * 3 + [col] * 4,
        ),
        out_shape=[pltpu.HBM(queries.shape, BF), pltpu.HBM(pair, F32)]
        + [pltpu.HBM(pair, BF)] * 3
        + [pltpu.HBM(queries.shape, BF)] * 4,
        compiler_params=params(),
        cost_estimate=pl.CostEstimate(flops=2 * 10**9, bytes_accessed=19 * 2**20, transcendentals=0),
        name="attend_back",
    )(meta, queries, grads, attended, probs, *keys, *values)


def project_back_kernel(g, w, out):
    out[...] = dot(g[...], w[...], NT).astype(BF)


def project_back(grads, weight):
    tokens = grads.shape[0]
    tile = 256
    return pl.pallas_call(
        project_back_kernel,
        grid=(weight.shape[0] // tile,),
        in_specs=[
            pl.BlockSpec(grads.shape, lambda i: (0, 0)),
            pl.BlockSpec((tile, weight.shape[1]), lambda i: (i, 0)),
        ],
        out_specs=pl.BlockSpec((tokens, tile), lambda i: (0, i)),
        out_shape=jax.ShapeDtypeStruct((tokens, weight.shape[0]), BF),
        compiler_params=params(),
        cost_estimate=pl.CostEstimate(flops=2 * 10**9, bytes_accessed=10 * 2**20, transcendentals=0),
        name="project_back",
    )(grads, weight)


def project_kernel(a, w, out):
    out[...] = dot(a[...], w[...], NN).astype(BF)


def project(attended, weight):
    tokens, depth = attended.shape
    wide = weight.shape[1] // GROUPS
    tile = 512
    steps = wide // tile
    return pl.pallas_call(
        project_kernel,
        grid=(GROUPS * steps,),
        in_specs=[
            pl.BlockSpec((tokens, depth), lambda i: (0, 0)),
            pl.BlockSpec((depth, tile), lambda i: (0, i)),
        ],
        out_specs=pl.BlockSpec((tokens, tile), lambda i: (i // steps, i % steps)),
        out_shape=jax.ShapeDtypeStruct((GROUPS * tokens, wide), BF),
        compiler_params=params(),
        cost_estimate=pl.CostEstimate(flops=2 * 10**9, bytes_accessed=11 * 2**20, transcendentals=0),
        name="project",
    )(attended, weight)


def nothing(*refs):
    pass


def after(value, *others, flops=0):
    anywhere = pl.BlockSpec(memory_space=pl.ANY)
    return pl.pallas_call(
        nothing,
        in_specs=[anywhere] * (1 + len(others)),
        out_specs=anywhere,
        out_shape=jax.ShapeDtypeStruct(value.shape, value.dtype),
        input_output_aliases={0: 0},
        cost_estimate=pl.CostEstimate(flops=flops, bytes_accessed=0, transcendentals=0),
        name="after",
    )(value, *others)


def body(queries, keys, values, layout, out_weight, out_grad):
    position = lax.axis_index("seq").astype(jnp.int32)
    meta = jnp.concatenate([layout.reshape(-1), position[None]])
    octet = position // 8
    core = position % 2

    def roots(own):
        return (
            move(own, lambda r: r + 8 if x_of(r) < 3 else None),
            move(own, lambda r: r + 2 if r % 8 < 6 else None),
            move(own, lambda r: r + 4 if r % 8 < 4 else None),
        )

    def wraps(own, r8o, r2o, r4o, crossed, *others, flops=0):
        r8w = move(crossed, lambda r: r - 8 if 40 <= r < 48 else None)
        r8 = jnp.where(octet == 4, r8w, r8o)
        r2w = move(r8, lambda r: r - 6 if r % 8 >= 6 else None)
        r4w = move(r8, lambda r: r - 4 if r % 8 >= 4 else None)
        r1 = after(jnp.where(core == 0, own, r2o + r2w), r4w, *others, flops=flops)
        return move(r1, lambda r: r ^ 1), r2o, r2w, r4o, r4w, r8

    k16 = move(keys, lambda r: r + 16 if r < 48 else None)
    v16a = move(values, lambda r: (r & 32) | ((r + 16) & 31) if r < 48 else None)
    k_roots = roots(keys)
    v_roots = roots(values)
    v16z = after(move(v16a, lambda r: r + 32 if r < 16 else None), flops=10**10)
    k16 = after(k16, *k_roots)
    key_set = (keys,) + wraps(keys, *k_roots, k16, flops=10**10) + (k16,)
    full_grad = lax.all_gather(after(out_grad, v16z, key_set[6]), "head", axis=1, tiled=True)
    value_set = (values,) + wraps(values, *v_roots, v16z, key_set[1]) + (v16a, v16z)
    probs, attended = forward(meta, queries, key_set, value_set)
    grad_attn = project_back(after(full_grad, attended), out_weight)
    dq, own, g1, g2, g4, k8, v8, k16, v16 = backward(
        meta, queries, grad_attn, attended, probs, key_set, value_set
    )
    crossing = lambda r: r - 16 if 32 <= r < 48 else None
    within = lambda r: r - 16 if x_of(r) >= 2 else None
    near = lambda r: r - 8 if x_of(r) > 0 else None
    s1 = move(g1, lambda r: r ^ 1)
    w4 = move(g4, lambda r: r + 4 if r % 8 < 4 else None)
    xv16 = move(v16, lambda r: r + 16 if 32 <= r < 48 else None)
    zk16 = move(k16, crossing)
    g2 = g2 + jnp.where(core == 1, s1, 0)
    w2 = move(g2, lambda r: r + 6 if r % 8 < 2 else None)
    partial = project(after(attended, g2), out_weight)
    mixed = lax.psum_scatter(partial, "head", scatter_dimension=0, tiled=True)
    zv16 = move(xv16, lambda r: r - 32 if r >= 48 else None)
    h4 = move(g4, lambda r: r - 4 if r % 8 >= 4 else None)
    h2 = move(g2, lambda r: r - 2 if r % 8 >= 2 else None)
    h16 = [move(k16, within), move(v16, within)]
    w2 = after(w2, w4, zk16, zv16, flops=4 * 10**10)
    k8 = (k8.astype(F32) + w2[0].astype(F32) + w4[0].astype(F32)).astype(BF)
    v8 = (v8.astype(F32) + w2[1].astype(F32) + w4[1].astype(F32)).astype(BF)
    xv8 = move(v8, lambda r: r + 24 if 32 <= r < 40 else None)
    zk8 = move(k8, lambda r: r - 8 if 32 <= r < 40 else None)
    h8 = [move(k8, near), move(v8, near)]
    xv8 = after(xv8, h4, *h16)
    zv8 = move(xv8, lambda r: r - 32 if r >= 56 else None)
    early = own + jnp.where(core == 0, s1, 0).astype(F32) + h4.astype(F32) + h2.astype(F32)
    totals = []
    for t, terms in ((0, (zk16, h16[0], h8[0], zk8)), (1, (zv16, h16[1], h8[1], zv8))):
        total = early[t]
        for term in terms:
            total = total + term.astype(F32)
        totals.append(total.astype(BF))
    return mixed, dq, totals[0], totals[1]


def solution(mesh):
    placed = (
        P("seq", "head"),
        P("seq", "head"),
        P("seq", "head"),
        P("seq", None),
        P("head", None),
        P("seq", "head"),
    )
    return jax.shard_map(
        body,
        mesh=mesh,
        in_specs=placed,
        out_specs=(P("seq", "head"), P("seq", "head"), P("seq", "head"), P("seq", "head")),
        check_vma=False,
    )
```

```python
import math

import jax
import jax.numpy as jnp
from jax import lax
from jax.experimental import pallas as pl
from jax.experimental.pallas import tpu as pltpu
from jax.sharding import PartitionSpec as P

HD = 128
BT = 128
LEVELS = 5
SCALE = 1.0 / math.sqrt(HD)
LOG2E = 1.0 / math.log(2.0)
NEG = -1e30
BF = jnp.bfloat16
F32 = jnp.float32
RUNS = 64
GROUPS = 4
STEP = 2
NT = (((1,), (1,)), ((), ()))
NN = (((1,), (0,)), ((), ()))
TN = (((0,), (0,)), ((), ()))


def params(mib=48):
    return pltpu.CompilerParams(vmem_limit_bytes=mib * 1024 * 1024)


def dot(a, b, dims):
    return lax.dot_general(a, b, dims, preferred_element_type=F32)


def move(value, target):
    pairs = [(r, target(r)) for r in range(RUNS)]
    return lax.ppermute(value, "seq", [(a, b) for a, b in pairs if b is not None])


def x_of(r):
    return (r >> 3) & 3


KEY_REFS = (1, 1, 2, 2, 1, 1)
VALUE_REFS = (1, 1, 2, 2, 1, 2)


def grouped(refs, counts):
    groups, at = [], 0
    for count in counts:
        groups.append(refs[at : at + count])
        at += count
    return groups


def gather_blocks(meta, groups, b, cols):
    blocks = [groups[0][0][b * BT : (b + 1) * BT, cols]]
    for j in range(LEVELS):
        rows = pl.ds(pl.multiple_of(meta[b * LEVELS + j] * BT, BT), BT)
        block = groups[1 + j][0][rows, cols]
        if len(groups[1 + j]) == 2:
            block = block + groups[1 + j][1][rows, cols]
        blocks.append(block)
    return jnp.concatenate(blocks, axis=0)


def forward_kernel(meta, q, *refs):
    keys, values = grouped(refs[:8], KEY_REFS), grouped(refs[8:17], VALUE_REFS)
    p_out, o_out = refs[17:]
    position = meta[2 * LEVELS]
    rows = lax.broadcasted_iota(jnp.int32, (BT, BT), 0)
    cols = lax.broadcasted_iota(jnp.int32, (BT, BT), 1)
    for h, b in [(h, b) for h in range(STEP) for b in range(2)]:
        mine = slice(b * BT, (b + 1) * BT)
        here = slice(h * HD, (h + 1) * HD)
        s = dot(q[mine, here], gather_blocks(meta, keys, b, here), NT)
        parts = [jnp.where(rows >= cols, s[:, :BT], NEG)]
        for j in range(LEVELS):
            parts.append(jnp.where(position >= 2**j, s[:, (j + 1) * BT : (j + 2) * BT], NEG))
        s = jnp.concatenate(parts, axis=1)
        peak = jnp.max(s, axis=1, keepdims=True)
        e = jnp.exp2((s - peak) * (SCALE * LOG2E))
        p = (e * (1.0 / jnp.sum(e, axis=1, keepdims=True))).astype(BF)
        p_out[h, mine, :] = p
        o_out[mine, here] = dot(p, gather_blocks(meta, values, b, here), NN).astype(BF)


def forward(meta, queries, keys, values):
    heads = queries.shape[1] // HD
    col = pl.BlockSpec((2 * BT, STEP * HD), lambda h, m: (0, h))
    return pl.pallas_call(
        forward_kernel,
        grid_spec=pltpu.PrefetchScalarGridSpec(
            num_scalar_prefetch=1,
            grid=(heads // STEP,),
            in_specs=[col] * 18,
            out_specs=[pl.BlockSpec((STEP, 2 * BT, 6 * BT), lambda h, m: (h, 0, 0)), col],
        ),
        out_shape=[
            jax.ShapeDtypeStruct((heads, 2 * BT, 6 * BT), BF),
            jax.ShapeDtypeStruct(queries.shape, BF),
        ],
        compiler_params=params(),
        cost_estimate=pl.CostEstimate(flops=10**9, bytes_accessed=9 * 2**20, transcendentals=10**6),
        name="attend",
    )(meta, queries, *keys, *values)


def backward_kernel(meta, q, g, o, p_in, *refs):
    keys, values = grouped(refs[:8], KEY_REFS), grouped(refs[8:17], VALUE_REFS)
    (dq_out, own_out), sends = refs[17:19], refs[19:]
    for h in range(STEP):
        here = slice(h * HD, (h + 1) * HD)
        halves = []
        for b in range(2):
            mine = slice(b * BT, (b + 1) * BT)
            gb = g[mine, here]
            qb = q[mine, here]
            correction = jnp.sum(gb.astype(F32) * o[mine, here].astype(F32), axis=1, keepdims=True)
            p = p_in[h, mine, :]
            dp = dot(gb, gather_blocks(meta, values, b, here), NT)
            ds = (p.astype(F32) * (dp - correction) * SCALE).astype(BF)
            dq_out[mine, here] = dot(ds, gather_blocks(meta, keys, b, here), NN).astype(BF)
            dk = dot(ds, qb, TN)
            dv = dot(p, gb, TN)
            own_out[0, mine, here] = dk[:BT]
            own_out[1, mine, here] = dv[:BT]
            halves.append((dk, dv))
        for j in range(LEVELS):
            part = slice((j + 1) * BT, (j + 2) * BT)
            for t in range(2):
                for slot in range(2):
                    total = jnp.where(meta[j] == slot, halves[0][t][part], 0.0) + jnp.where(
                        meta[LEVELS + j] == slot, halves[1][t][part], 0.0
                    )
                    rows = slice(slot * BT, (slot + 1) * BT)
                    if j < 3:
                        sends[j][t, rows, here] = total.astype(BF)
                    else:
                        sends[3 + 2 * (j - 3) + t][rows, here] = total.astype(BF)


def backward(meta, queries, grads, attended, probs, keys, values):
    heads = queries.shape[1] // HD
    col = pl.BlockSpec((2 * BT, STEP * HD), lambda h, m: (0, h))
    both = pl.BlockSpec((2, 2 * BT, STEP * HD), lambda h, m: (0, 0, h))
    pair = (2,) + queries.shape
    return pl.pallas_call(
        backward_kernel,
        grid_spec=pltpu.PrefetchScalarGridSpec(
            num_scalar_prefetch=1,
            grid=(heads // STEP,),
            in_specs=[col] * 3
            + [pl.BlockSpec((STEP, 2 * BT, 6 * BT), lambda h, m: (h, 0, 0))]
            + [col] * 17,
            out_specs=[col, both] + [both] * 3 + [col] * 4,
        ),
        out_shape=[pltpu.HBM(queries.shape, BF), pltpu.HBM(pair, F32)]
        + [pltpu.HBM(pair, BF)] * 3
        + [pltpu.HBM(queries.shape, BF)] * 4,
        compiler_params=params(),
        cost_estimate=pl.CostEstimate(flops=2 * 10**9, bytes_accessed=19 * 2**20, transcendentals=0),
        name="attend_back",
    )(meta, queries, grads, attended, probs, *keys, *values)


def project_back_kernel(g, w, out):
    out[...] = dot(g[...], w[...], NT).astype(BF)


def project_back(grads, weight):
    tokens = grads.shape[0]
    tile = 256
    return pl.pallas_call(
        project_back_kernel,
        grid=(weight.shape[0] // tile,),
        in_specs=[
            pl.BlockSpec(grads.shape, lambda i: (0, 0)),
            pl.BlockSpec((tile, weight.shape[1]), lambda i: (i, 0)),
        ],
        out_specs=pl.BlockSpec((tokens, tile), lambda i: (0, i)),
        out_shape=jax.ShapeDtypeStruct((tokens, weight.shape[0]), BF),
        compiler_params=params(),
        cost_estimate=pl.CostEstimate(flops=2 * 10**9, bytes_accessed=10 * 2**20, transcendentals=0),
        name="project_back",
    )(grads, weight)


def project_kernel(a, w, out):
    out[...] = dot(a[...], w[...], NN).astype(BF)


def project(attended, weight):
    tokens, depth = attended.shape
    wide = weight.shape[1] // GROUPS
    tile = 512
    steps = wide // tile
    return pl.pallas_call(
        project_kernel,
        grid=(GROUPS * steps,),
        in_specs=[
            pl.BlockSpec((tokens, depth), lambda i: (0, 0)),
            pl.BlockSpec((depth, tile), lambda i: (0, i)),
        ],
        out_specs=pl.BlockSpec((tokens, tile), lambda i: (i // steps, i % steps)),
        out_shape=jax.ShapeDtypeStruct((GROUPS * tokens, wide), BF),
        compiler_params=params(),
        cost_estimate=pl.CostEstimate(flops=2 * 10**9, bytes_accessed=11 * 2**20, transcendentals=0),
        name="project",
    )(attended, weight)


def nothing(*refs):
    pass


def after(value, *others, flops=0):
    anywhere = pl.BlockSpec(memory_space=pl.ANY)
    return pl.pallas_call(
        nothing,
        in_specs=[anywhere] * (1 + len(others)),
        out_specs=anywhere,
        out_shape=jax.ShapeDtypeStruct(value.shape, value.dtype),
        input_output_aliases={0: 0},
        cost_estimate=pl.CostEstimate(flops=flops, bytes_accessed=0, transcendentals=0),
        name="after",
    )(value, *others)


def body(queries, keys, values, layout, out_weight, out_grad):
    position = lax.axis_index("seq").astype(jnp.int32)
    meta = jnp.concatenate([layout.reshape(-1), position[None]])
    octet = position // 8
    core = position % 2

    def roots(own):
        return (
            move(own, lambda r: r + 8 if x_of(r) < 3 else None),
            move(own, lambda r: r + 2 if r % 8 < 6 else None),
            move(own, lambda r: r + 4 if r % 8 < 4 else None),
        )

    def wraps(own, r8o, r2o, r4o, crossed, *others, flops=0):
        r8w = move(crossed, lambda r: r - 8 if 40 <= r < 48 else None)
        r8 = jnp.where(octet == 4, r8w, r8o)
        r2w = move(r8, lambda r: r - 6 if r % 8 >= 6 else None)
        r4w = move(r8, lambda r: r - 4 if r % 8 >= 4 else None)
        r1 = after(jnp.where(core == 0, own, r2o + r2w), r4w, *others, flops=flops)
        return move(r1, lambda r: r ^ 1), r2o, r2w, r4o, r4w, r8

    k16 = move(keys, lambda r: r + 16 if r < 48 else None)
    v16a = move(values, lambda r: (r & 32) | ((r + 16) & 31) if r < 48 else None)
    k_roots = roots(keys)
    v_roots = roots(values)
    v16z = after(move(v16a, lambda r: r + 32 if r < 16 else None), flops=10**10)
    k16 = after(k16, *k_roots)
    key_set = (keys,) + wraps(keys, *k_roots, k16, flops=10**10) + (k16,)
    full_grad = lax.all_gather(after(out_grad, v16z, key_set[6]), "head", axis=1, tiled=True)
    value_set = (values,) + wraps(values, *v_roots, v16z, key_set[1]) + (v16a, v16z)
    probs, attended = forward(meta, queries, key_set, value_set)
    probs = after(probs, flops=4 * 10**9)
    grad_attn = project_back(after(full_grad, probs), out_weight)
    dq, own, g1, g2, g4, k8, v8, k16, v16 = backward(
        meta, queries, grad_attn, attended, probs, key_set, value_set
    )
    crossing = lambda r: r - 16 if 32 <= r < 48 else None
    within = lambda r: r - 16 if x_of(r) >= 2 else None
    near = lambda r: r - 8 if x_of(r) > 0 else None
    s1 = move(g1, lambda r: r ^ 1)
    w4 = move(g4, lambda r: r + 4 if r % 8 < 4 else None)
    xv16 = move(v16, lambda r: r + 16 if 32 <= r < 48 else None)
    zk16 = move(k16, crossing)
    g2 = g2 + jnp.where(core == 1, s1, 0)
    w2 = move(g2, lambda r: r + 6 if r % 8 < 2 else None)
    partial = project(after(attended, g2), out_weight)
    mixed = lax.psum_scatter(partial, "head", scatter_dimension=0, tiled=True)
    zv16 = move(xv16, lambda r: r - 32 if r >= 48 else None)
    h4 = move(g4, lambda r: r - 4 if r % 8 >= 4 else None)
    h2 = move(g2, lambda r: r - 2 if r % 8 >= 2 else None)
    h16 = [move(k16, within), move(v16, within)]
    w2 = after(w2, w4, zk16, zv16, flops=4 * 10**10)
    k8 = (k8.astype(F32) + w2[0].astype(F32) + w4[0].astype(F32)).astype(BF)
    v8 = (v8.astype(F32) + w2[1].astype(F32) + w4[1].astype(F32)).astype(BF)
    xv8 = move(v8, lambda r: r + 24 if 32 <= r < 40 else None)
    zk8 = move(k8, lambda r: r - 8 if 32 <= r < 40 else None)
    h8 = [move(k8, near), move(v8, near)]
    xv8 = after(xv8, h4, *h16)
    zv8 = move(xv8, lambda r: r - 32 if r >= 56 else None)
    early = own + jnp.where(core == 0, s1, 0).astype(F32) + h4.astype(F32) + h2.astype(F32)
    totals = []
    for t, terms in ((0, (zk16, h16[0], h8[0], zk8)), (1, (zv16, h16[1], h8[1], zv8))):
        total = early[t]
        for term in terms:
            total = total + term.astype(F32)
        totals.append(total.astype(BF))
    return mixed, dq, totals[0], totals[1]


def solution(mesh):
    placed = (
        P("seq", "head"),
        P("seq", "head"),
        P("seq", "head"),
        P("seq", None),
        P("head", None),
        P("seq", "head"),
    )
    return jax.shard_map(
        body,
        mesh=mesh,
        in_specs=placed,
        out_specs=(P("seq", "head"), P("seq", "head"), P("seq", "head"), P("seq", "head")),
        check_vma=False,
    )
```
